32 devices in a mesh: ctx: 8 (over z, core), head: 4 (over y, x).
Axes of the slice: x: 2, y: 2, z: 4, core: 2. Of those that a mesh axis runs over, the one named last changes fastest.
Arguments:
- queries: bfloat16 [512, 16384], P('ctx', 'head'), may hold values from -8000 to 8000
- key_codes: bfloat16 [16384, 1024], P('ctx', 'head'), may hold values from -127 to 127
- value_codes: bfloat16 [16384, 1024], P('ctx', 'head'), may hold values from -127 to 127
- key_scales: int32 [256, 8], P('ctx', 'head'), may hold values from 1 to 16
- value_scales: int32 [256, 8], P('ctx', 'head'), may hold values from 1 to 16
- positions: int32 [512], replicated, may hold values from 0 to 16383
- out_weight: bfloat16 [16384, 16384], P('head', 'ctx'), may hold values from -0.046875 to 0.046875
Outputs:
- projected: bfloat16 [512, 16384], P('head', 'ctx')
The draws below stay inside these ranges and needn't reach their ends.
All inputs are finite; a program needn't handle non-finite values.
Results may differ from the reference program's by a relative error of at most 0.009.
Values may be sent and summed in bfloat16 or wider, within the bound.
A program may use at most 128 MiB of HBM per device.

```python
import math
import jax
import jax.numpy as jnp
from jax import lax

D = 16384
QH = 128
KVH = 8
HD = 128
BLOCK = 64
CTX = 16384
QROWS = 512


def shared_codes(key):
    return jax.random.randint(jax.random.fold_in(key, 11), (CTX, KVH * HD), -127, 128)


def shared_positions(key):
    return jax.random.randint(jax.random.fold_in(key, 12), (QROWS,), 0, CTX)


def draw_key_codes(key, part):
    return shared_codes(key).astype(jnp.float32).astype(jnp.bfloat16)


def draw_value_codes(key, part):
    code_table = jax.random.randint(jax.random.fold_in(key, 13), (CTX, KVH * HD), -127, 128)
    return code_table.astype(jnp.float32).astype(jnp.bfloat16)


def draw_positions(key, part):
    return shared_positions(key)


def draw_queries(key, part):
    gaussian = jax.random.normal(jax.random.fold_in(key, 14), (QROWS, QH * HD), jnp.float32)
    return gaussian.astype(jnp.bfloat16)


def set_ends(entries, stream_key, least, top_value):
    dims = entries.shape
    place = [jax.random.randint(jax.random.fold_in(stream_key, axis), (), 0, dims[axis]) for axis in range(len(dims))]
    entries = entries.at[tuple(place)].set(least)
    longest = dims.index(max(dims))
    place[longest] = (place[longest] + 1) % dims[longest]
    return entries.at[tuple(place)].set(top_value)


def block_scale(own_key, extent, split, least, top_value):
    gain = 1.0
    for dim, shards_of in split:
        heights = jax.random.uniform(jax.random.fold_in(jax.random.fold_in(own_key, 6), dim), (shards_of,), jnp.float32, least / len(split), top_value / len(split))
        gain = gain * jnp.repeat(jnp.exp(heights), extent[dim] // shards_of).reshape((-1,) + (1,) * (len(extent) - 1 - dim))
    return gain


def bell_draw(rng, shape, spread, most, cuts=(), kind=jnp.bfloat16):
    result = spread * jax.random.normal(rng, shape, jnp.float32)
    if cuts:
        result = result * block_scale(rng, shape, cuts, -0.22, 0.18)
    return jnp.clip(result, -most, most).astype(kind)


def setup_inputs(seed: int = 0) -> dict:
    arg_keys = jax.random.split(jax.random.key(seed), 8)
    return {
        "queries": draw_queries(jax.random.fold_in(arg_keys[7], 71), 0),
        "key_codes": draw_key_codes(jax.random.fold_in(arg_keys[7], 71), 0),
        "value_codes": draw_value_codes(jax.random.fold_in(arg_keys[7], 71), 0),
        "key_scales": set_ends(jax.random.randint(arg_keys[3], (CTX // BLOCK, KVH), 1, 17), jax.random.fold_in(arg_keys[3], 1), 1, 16).astype(jnp.int32),
        "value_scales": set_ends(jax.random.randint(arg_keys[4], (CTX // BLOCK, KVH), 1, 17), jax.random.fold_in(arg_keys[4], 1), 1, 16).astype(jnp.int32),
        "positions": draw_positions(jax.random.fold_in(arg_keys[7], 71), 0),
        "out_weight": bell_draw(arg_keys[6], (QH * HD, D), (QH * HD) ** -0.5, 0.046875, ((0, 4), (1, 8))),
    }


QUANT_STEP = 1.0 / 2048.0
MASKED = -1e+30

def hadamard_signs(size_value):
    indices = jnp.arange(size_value, dtype=jnp.int32)
    common = jnp.bitwise_and(indices[:, None], indices[None, :])
    parity = jnp.zeros((size_value, size_value), jnp.int32)
    for shift_bit in range(max(int(size_value).bit_length(), 1)):
        parity = jnp.bitwise_xor(parity, jnp.bitwise_and(jnp.right_shift(common, shift_bit), 1))
    return 1.0 - 2.0 * parity.astype(jnp.float32)

def reference(queries, key_codes, value_codes, key_scales, value_scales, positions, out_weight):
    signs = hadamard_signs(HD)
    group_size = QH // KVH
    query_heads = queries.reshape(QROWS, QH, HD).astype(jnp.float32)
    rotated = jnp.einsum('rhd,de->rhe', query_heads, signs, precision=lax.Precision.HIGHEST) / math.sqrt(HD)
    key_factor = jnp.repeat(key_scales.astype(jnp.float32), BLOCK, axis=0) * (QUANT_STEP / math.sqrt(HD))
    value_factor = jnp.repeat(value_scales.astype(jnp.float32), BLOCK, axis=0) * QUANT_STEP
    key_pos = jnp.arange(CTX, dtype=jnp.int32)
    visible = key_pos[None, :] <= positions[:, None]

    def one_head(head_index):
        kv_index = head_index // group_size
        query_rows = lax.dynamic_index_in_dim(rotated, head_index, 1, keepdims=False)
        key_block = lax.dynamic_slice_in_dim(key_codes, (kv_index * HD).astype(jnp.int32), HD, 1).astype(jnp.float32)
        value_block = lax.dynamic_slice_in_dim(value_codes, (kv_index * HD).astype(jnp.int32), HD, 1)
        key_scale = lax.dynamic_index_in_dim(key_factor, kv_index, 1, keepdims=False)
        value_scale = lax.dynamic_index_in_dim(value_factor, kv_index, 1, keepdims=False)
        scores = jnp.dot(query_rows, key_block.T, preferred_element_type=jnp.float32, precision=lax.Precision.HIGHEST) * key_scale[None, :]
        scores = jnp.where(visible, scores, MASKED)
        highest = lax.optimization_barrier(jnp.max(scores, axis=1, keepdims=True))
        probs = jnp.where(visible, jnp.exp(scores - highest), 0.0)
        row_total = lax.optimization_barrier(jnp.sum(probs, axis=1, keepdims=True))
        weights = (probs * value_scale[None, :]).astype(jnp.bfloat16)
        numerator = jnp.dot(weights, value_block, preferred_element_type=jnp.float32)
        return (numerator / row_total).astype(jnp.bfloat16)
    normalized = lax.map(one_head, jnp.arange(QH, dtype=jnp.int32))
    attention = (jnp.einsum('hrd,de->hre', normalized.astype(jnp.float32), signs) / math.sqrt(HD)).astype(jnp.bfloat16)
    attention = jnp.transpose(attention, (1, 0, 2)).reshape(QROWS, QH * HD)
    return jnp.dot(attention, out_weight, preferred_element_type=jnp.float32).astype(jnp.bfloat16)
```

```python
import functools
import math

import jax
import jax.numpy as jnp
from jax import lax
from jax.experimental import pallas as pl
from jax.experimental.pallas import tpu as pltpu
from jax.sharding import PartitionSpec as P

HD = 128
BLOCK = 64
QUANT_STEP = 1.0 / 2048.0
MASKED = -1e30
LANES = 128


def hadamard_signs(size_value):
    indices = jnp.arange(size_value, dtype=jnp.int32)
    common = jnp.bitwise_and(indices[:, None], indices[None, :])
    parity = jnp.zeros((size_value, size_value), jnp.int32)
    for shift_bit in range(max(int(size_value).bit_length(), 1)):
        parity = jnp.bitwise_xor(parity, jnp.bitwise_and(jnp.right_shift(common, shift_bit), 1))
    return 1.0 - 2.0 * parity.astype(jnp.float32)


def attend_kernel(heads, group, q_ref, kk_ref, vv_ref, scale_ref, pos_ref, o_ref, top_ref, total_ref, s_a, s_b):
    rows, ctx = s_a.shape
    lane = lax.broadcasted_iota(jnp.int32, (rows, LANES), 1)

    def scores(h, s_ref):
        g = h // group
        col = pl.multiple_of(h * HD, HD)
        q = q_ref[:, pl.ds(col, HD)]
        s = jnp.dot(jnp.concatenate([q, q], axis=1), kk_ref[g], preferred_element_type=jnp.float32)
        where = lax.broadcasted_iota(jnp.int32, (rows, ctx), 1)
        s = jnp.where(where <= pos_ref[...], s * scale_ref[g], MASKED)
        s_ref[...] = s
        return jnp.max(s, axis=1, keepdims=True)

    def values(h, s_ref, top):
        g = h // group
        col = pl.multiple_of(h * HD, HD)
        p = jnp.exp2(s_ref[...] - top).astype(jnp.bfloat16)
        both = jnp.dot(p, vv_ref[g], preferred_element_type=jnp.float32)
        total = both[:, HD:]
        o_ref[:, pl.ds(col, HD)] = (both[:, :HD] / total).astype(jnp.bfloat16)
        top_ref[...] = jnp.where(lane == h, top, top_ref[...])
        total_ref[...] = jnp.where(lane == h, total, total_ref[...])

    top_ref[...] = jnp.zeros_like(top_ref)
    total_ref[...] = jnp.zeros_like(total_ref)
    first = scores(0, s_a)

    def step(i, top_a):
        h = i * 2
        top_b = scores(h + 1, s_b)
        values(h, s_a, top_a)
        later = scores(jnp.minimum(h + 2, heads - 1), s_a)
        values(h + 1, s_b, top_b)
        return later

    lax.fori_loop(0, heads // 2, step, first)


def attend(queries, kk, vv, scale, limit, heads, group):
    rows, width = queries.shape
    kv, depth, ctx = kk.shape
    block = min(256, rows)
    whole = lambda r: (0, 0, 0)
    stats = jax.ShapeDtypeStruct((rows, LANES), jnp.float32)
    return pl.pallas_call(
        functools.partial(attend_kernel, heads, group),
        grid=(rows // block,),
        in_specs=[
            pl.BlockSpec((block, width), lambda r: (r, 0)),
            pl.BlockSpec((kv, depth, ctx), whole),
            pl.BlockSpec((kv, ctx, 2 * HD), whole),
            pl.BlockSpec((kv, 1, ctx), whole),
            pl.BlockSpec((block, 1), lambda r: (r, 0)),
        ],
        out_specs=[
            pl.BlockSpec((block, width), lambda r: (r, 0)),
            pl.BlockSpec((block, LANES), lambda r: (r, 0)),
            pl.BlockSpec((block, LANES), lambda r: (r, 0)),
        ],
        out_shape=[jax.ShapeDtypeStruct((rows, width), jnp.bfloat16), stats, stats],
        scratch_shapes=[pltpu.VMEM((block, ctx), jnp.float32)] * 2,
        compiler_params=pltpu.CompilerParams(vmem_limit_bytes=48 * 1024 * 1024),
        cost_estimate=pl.CostEstimate(
            flops=6 * rows * width * ctx, bytes_accessed=4 * rows * width, transcendentals=rows * heads * ctx
        ),
    )(queries, kk, vv, scale, limit)


def on_device(queries, key_codes, value_codes, key_scales, value_scales, positions, out_weight):
    q_rows = queries.shape[0]
    kv_local = key_scales.shape[1]
    ctx_local = key_codes.shape[0]
    heads_local = queries.shape[1] // HD
    group_size = heads_local // kv_local
    cycle_index = lax.axis_index("ctx")
    cycle_size = lax.axis_size("ctx")
    signs = hadamard_signs(HD)
    every_query = lax.all_gather(queries, "ctx", axis=0, tiled=True)
    keys = key_codes.reshape(ctx_local, kv_local, HD)
    turned = jnp.einsum(
        "cgd,de->gec", keys, signs.astype(jnp.bfloat16), preferred_element_type=jnp.float32
    )
    coarse = jnp.floor(turned * (1.0 / 128.0)) * 128.0
    kk = jnp.concatenate([coarse, turned - coarse], axis=1).astype(jnp.bfloat16)
    scale = jnp.repeat(key_scales.astype(jnp.float32), BLOCK, axis=0).T[:, None, :]
    scale = scale * (QUANT_STEP / HD * math.log2(math.e))
    value_factor = jnp.repeat(value_scales.astype(jnp.float32), BLOCK, axis=0) * QUANT_STEP
    scaled = value_codes.reshape(ctx_local, kv_local, HD).astype(jnp.float32) * value_factor[..., None]
    vv = jnp.concatenate([scaled, jnp.ones_like(scaled)], axis=2).astype(jnp.bfloat16)
    vv = vv.transpose(1, 0, 2)
    limit = (positions - cycle_index * ctx_local)[:, None]
    part, top, total = attend(every_query, kk, vv, scale, limit, heads_local, group_size)

    part = lax.all_to_all(part, "ctx", 0, 0, tiled=True).reshape(cycle_size, q_rows, heads_local, HD)
    stats = jnp.concatenate([top[:, :heads_local], total[:, :heads_local]], axis=1)
    stats = lax.all_to_all(stats, "ctx", 0, 0, tiled=True).reshape(cycle_size, q_rows, 2, heads_local)
    top, total = stats[:, :, 0], stats[:, :, 1]
    share = total * jnp.exp2(top - jnp.max(top, axis=0, keepdims=True))
    share = share / jnp.sum(share, axis=0, keepdims=True)
    normalized = jnp.sum(part.astype(jnp.float32) * share[..., None], axis=0).astype(jnp.bfloat16)
    restored = jnp.einsum(
        "rhd,de->rhe", normalized, signs.astype(jnp.bfloat16), preferred_element_type=jnp.float32
    )
    attention = (restored / math.sqrt(HD)).astype(jnp.bfloat16).reshape(q_rows, heads_local * HD)
    attention_rows = lax.all_gather(attention, "ctx", axis=0, tiled=True)
    projected = lax.psum_scatter(
        jnp.dot(attention_rows, out_weight, preferred_element_type=jnp.float32),
        "head",
        scatter_dimension=0,
        tiled=True,
    )
    return projected.astype(jnp.bfloat16)


def solution(mesh):
    in_specs = (
        P("ctx", "head"),
        P("ctx", "head"),
        P("ctx", "head"),
        P("ctx", "head"),
        P("ctx", "head"),
        P(),
        P("head", "ctx"),
    )
    out_specs = P("head", "ctx")
    return jax.shard_map(
        on_device, mesh=mesh, in_specs=in_specs, out_specs=out_specs, check_vma=False
    )
```

```python
import functools
import math

import jax
import jax.numpy as jnp
from jax import lax
from jax.experimental import pallas as pl
from jax.experimental.pallas import tpu as pltpu
from jax.sharding import PartitionSpec as P

HD = 128
BLOCK = 64
QUANT_STEP = 1.0 / 2048.0
MASKED = -1e30
LANES = 128
MESH = pl.DeviceIdType.MESH


def hadamard_signs(size_value):
    indices = jnp.arange(size_value, dtype=jnp.int32)
    common = jnp.bitwise_and(indices[:, None], indices[None, :])
    parity = jnp.zeros((size_value, size_value), jnp.int32)
    for shift_bit in range(max(int(size_value).bit_length(), 1)):
        parity = jnp.bitwise_xor(parity, jnp.bitwise_and(jnp.right_shift(common, shift_bit), 1))
    return 1.0 - 2.0 * parity.astype(jnp.float32)


def attend_kernel(heads, group, q_ref, kk_ref, vv_ref, scale_ref, pos_ref, o_ref, top_ref, total_ref, s_a, s_b):
    rows, ctx = s_a.shape
    lane = lax.broadcasted_iota(jnp.int32, (rows, LANES), 1)

    def scores(h, s_ref):
        g = h // group
        col = pl.multiple_of(h * HD, HD)
        q = q_ref[:, pl.ds(col, HD)]
        s = jnp.dot(jnp.concatenate([q, q], axis=1), kk_ref[g], preferred_element_type=jnp.float32)
        where = lax.broadcasted_iota(jnp.int32, (rows, ctx), 1)
        s = jnp.where(where <= pos_ref[...], s * scale_ref[g], MASKED)
        s_ref[...] = s
        return jnp.max(s, axis=1, keepdims=True)

    def values(h, s_ref, top):
        g = h // group
        col = pl.multiple_of(h * HD, HD)
        p = jnp.exp2(s_ref[...] - top).astype(jnp.bfloat16)
        both = jnp.dot(p, vv_ref[g], preferred_element_type=jnp.float32)
        total = both[:, HD:]
        o_ref[:, pl.ds(col, HD)] = (both[:, :HD] / total).astype(jnp.bfloat16)
        top_ref[...] = jnp.where(lane == h, top, top_ref[...])
        total_ref[...] = jnp.where(lane == h, total, total_ref[...])

    top_ref[...] = jnp.zeros_like(top_ref)
    total_ref[...] = jnp.zeros_like(total_ref)
    first = scores(0, s_a)

    def step(i, top_a):
        h = i * 2
        top_b = scores(h + 1, s_b)
        values(h, s_a, top_a)
        later = scores(jnp.minimum(h + 2, heads - 1), s_a)
        values(h + 1, s_b, top_b)
        return later

    lax.fori_loop(0, heads // 2, step, first)


def attend(queries, kk, vv, scale, limit, heads, group):
    rows, width = queries.shape
    kv, depth, ctx = kk.shape
    block = min(256, rows)
    whole = lambda r: (0, 0, 0)
    stats = jax.ShapeDtypeStruct((rows, LANES), jnp.float32)
    return pl.pallas_call(
        functools.partial(attend_kernel, heads, group),
        grid=(rows // block,),
        in_specs=[
            pl.BlockSpec((block, width), lambda r: (r, 0)),
            pl.BlockSpec((kv, depth, ctx), whole),
            pl.BlockSpec((kv, ctx, 2 * HD), whole),
            pl.BlockSpec((kv, 1, ctx), whole),
            pl.BlockSpec((block, 1), lambda r: (r, 0)),
        ],
        out_specs=[
            pl.BlockSpec((block, width), lambda r: (r, 0)),
            pl.BlockSpec((block, LANES), lambda r: (r, 0)),
            pl.BlockSpec((block, LANES), lambda r: (r, 0)),
        ],
        out_shape=[jax.ShapeDtypeStruct((rows, width), jnp.bfloat16), stats, stats],
        scratch_shapes=[pltpu.VMEM((block, ctx), jnp.float32)] * 2,
        compiler_params=pltpu.CompilerParams(vmem_limit_bytes=48 * 1024 * 1024),
        cost_estimate=pl.CostEstimate(
            flops=6 * rows * width * ctx, bytes_accessed=4 * rows * width, transcendentals=rows * heads * ctx
        ),
    )(queries, kk, vv, scale, limit)


def project_kernel(chips, parts, a_ref, w_hbm, o_ref, w_ref, att, own, out_part, in_part,
                   w_sem, send_z, recv_z, send_core, recv_core, send_head, recv_head):
    me = lax.axis_index("ctx")
    mine = lax.axis_index("head")
    chip, core = me // 2, lax.rem(me, 2)
    sibling = chip * 2 + 1 - core
    half = a_ref.shape[1]
    columns = w_ref.shape[1]
    tile = min(512, columns)
    load = pltpu.make_async_copy(w_hbm, w_ref, w_sem)
    load.start()

    barrier = pltpu.get_barrier_semaphore()
    pl.semaphore_signal(barrier, inc=1, device_id={"ctx": sibling}, device_id_type=MESH)
    for k in range(1, chips):
        other = lax.rem(chip + k, chips) * 2 + core
        pl.semaphore_signal(barrier, inc=1, device_id={"ctx": other}, device_id_type=MESH)
    for k in range(1, parts):
        other = lax.rem(mine + k, parts)
        pl.semaphore_signal(barrier, inc=1, device_id={"head": other}, device_id_type=MESH)
    pl.semaphore_wait(barrier, chips + parts - 1)

    def to_chip(k):
        return pltpu.make_async_remote_copy(
            src_ref=a_ref, dst_ref=att.at[chip, core],
            send_sem=send_z.at[k], recv_sem=recv_z.at[chips - k],
            device_id={"ctx": lax.rem(chip + k, chips) * 2 + core}, device_id_type=MESH)

    def from_chip(k):
        source = lax.rem(chip + k, chips)
        return pltpu.make_async_remote_copy(
            src_ref=a_ref, dst_ref=att.at[source, core],
            send_sem=send_z.at[k], recv_sem=recv_z.at[k],
            device_id={"ctx": source * 2 + core}, device_id_type=MESH)

    def to_core(k):
        source = lax.rem(chip + k, chips)
        return pltpu.make_async_remote_copy(
            src_ref=a_ref if k == 0 else att.at[source, core], dst_ref=att.at[source, core],
            send_sem=send_core.at[k], recv_sem=recv_core.at[k],
            device_id={"ctx": sibling}, device_id_type=MESH)

    def from_core(k):
        source = lax.rem(chip + k, chips)
        return pltpu.make_async_remote_copy(
            src_ref=a_ref, dst_ref=att.at[source, 1 - core],
            send_sem=send_core.at[k], recv_sem=recv_core.at[k],
            device_id={"ctx": sibling}, device_id_type=MESH)

    def to_part(k):
        block = lax.rem(chip + k, chips)
        return pltpu.make_async_remote_copy(
            src_ref=out_part.at[k], dst_ref=in_part.at[mine],
            send_sem=send_head.at[k], recv_sem=recv_head.at[mine],
            device_id={"head": block}, device_id_type=MESH)

    for k in range(1, chips):
        to_chip(k).start()
    to_core(0).start()
    att[chip, core] = a_ref[...]
    load.wait()
    for k in range(chips):
        if k > 0:
            from_chip(k).wait_recv()
            to_core(k).start()
        from_core(k).wait_recv()
        block = lax.rem(chip + k, chips)

        @pl.loop(0, columns // tile)
        def _(t):
            cols = pl.ds(pl.multiple_of(t * tile, tile), tile)
            product = jnp.dot(att[block, 0], w_ref[:half, cols], preferred_element_type=jnp.float32)
            product += jnp.dot(att[block, 1], w_ref[half:, cols], preferred_element_type=jnp.float32)
            out_part[k, :, cols] = product.astype(jnp.bfloat16)

            @pl.when(block == mine)
            def _():
                own[:, cols] = product

        @pl.when(block != mine)
        def _():
            to_part(k).start()

    total = own[...]
    for k in range(1, parts):
        source = lax.rem(mine + k, parts)
        pltpu.make_async_remote_copy(
            src_ref=out_part.at[0], dst_ref=in_part.at[source],
            send_sem=send_head.at[0], recv_sem=recv_head.at[source],
            device_id={"head": source}, device_id_type=MESH).wait_recv()
        total = total + in_part[source].astype(jnp.float32)
    o_ref[...] = total.astype(o_ref.dtype)
    for k in range(1, chips):
        to_chip(k).wait_send()
    for k in range(chips):
        to_core(k).wait_send()

        @pl.when(lax.rem(chip + k, chips) != mine)
        def _():
            to_part(k).wait_send()


def project(piece, out_weight, chips, parts):
    rows, half = piece.shape
    depth, columns = out_weight.shape
    dma = pltpu.SemaphoreType.DMA
    return pl.pallas_call(
        functools.partial(project_kernel, chips, parts),
        out_shape=jax.ShapeDtypeStruct((rows, columns), jnp.bfloat16),
        in_specs=[pl.BlockSpec(memory_space=pltpu.VMEM), pl.BlockSpec(memory_space=pl.ANY)],
        out_specs=pl.BlockSpec(memory_space=pltpu.VMEM),
        scratch_shapes=[
            pltpu.VMEM((depth, columns), jnp.bfloat16),
            pltpu.VMEM((chips, 2, rows, half), jnp.bfloat16),
            pltpu.VMEM((rows, columns), jnp.float32),
            pltpu.VMEM((chips, rows, columns), jnp.bfloat16),
            pltpu.VMEM((parts, rows, columns), jnp.bfloat16),
            dma,
            dma((chips,)), dma((chips,)), dma((chips,)), dma((chips,)),
            dma((chips,)), dma((parts,)),
        ],
        compiler_params=pltpu.CompilerParams(
            collective_id=1, has_side_effects=True, vmem_limit_bytes=50 * 1024 * 1024
        ),
        cost_estimate=pl.CostEstimate(
            flops=2 * chips * rows * depth * columns, bytes_accessed=2 * depth * columns, transcendentals=0
        ),
    )(piece, out_weight)


def on_device(queries, key_codes, value_codes, key_scales, value_scales, positions, out_weight):
    q_rows = queries.shape[0]
    kv_local = key_scales.shape[1]
    ctx_local = key_codes.shape[0]
    heads_local = queries.shape[1] // HD
    group_size = heads_local // kv_local
    cycle_index = lax.axis_index("ctx")
    cycle_size = lax.axis_size("ctx")
    signs = hadamard_signs(HD)
    every_query = lax.all_gather(queries, "ctx", axis=0, tiled=True)
    keys = key_codes.reshape(ctx_local, kv_local, HD)
    turned = jnp.einsum(
        "cgd,de->gec", keys, signs.astype(jnp.bfloat16), preferred_element_type=jnp.float32
    )
    coarse = jnp.floor(turned * (1.0 / 128.0)) * 128.0
    kk = jnp.concatenate([coarse, turned - coarse], axis=1).astype(jnp.bfloat16)
    scale = jnp.repeat(key_scales.astype(jnp.float32), BLOCK, axis=0).T[:, None, :]
    scale = scale * (QUANT_STEP / HD * math.log2(math.e))
    value_factor = jnp.repeat(value_scales.astype(jnp.float32), BLOCK, axis=0) * QUANT_STEP
    scaled = value_codes.reshape(ctx_local, kv_local, HD).astype(jnp.float32) * value_factor[..., None]
    vv = jnp.concatenate([scaled, jnp.ones_like(scaled)], axis=2).astype(jnp.bfloat16)
    vv = vv.transpose(1, 0, 2)
    limit = (positions - cycle_index * ctx_local)[:, None]
    part, top, total = attend(every_query, kk, vv, scale, limit, heads_local, group_size)

    part = lax.all_to_all(part, "ctx", 0, 0, tiled=True).reshape(cycle_size, q_rows, heads_local, HD)
    stats = jnp.concatenate([top[:, :heads_local], total[:, :heads_local]], axis=1)
    stats = lax.all_to_all(stats, "ctx", 0, 0, tiled=True).reshape(cycle_size, q_rows, 2, heads_local)
    top, total = stats[:, :, 0], stats[:, :, 1]
    share = total * jnp.exp2(top - jnp.max(top, axis=0, keepdims=True))
    share = share / jnp.sum(share, axis=0, keepdims=True)
    normalized = jnp.sum(part.astype(jnp.float32) * share[..., None], axis=0).astype(jnp.bfloat16)
    restored = jnp.einsum(
        "rhd,de->rhe", normalized, signs.astype(jnp.bfloat16), preferred_element_type=jnp.float32
    )
    attention = (restored / math.sqrt(HD)).astype(jnp.bfloat16).reshape(q_rows, heads_local * HD)
    half = attention.shape[1] // 2
    core = cycle_index % 2
    kept = lax.dynamic_slice_in_dim(attention, core * half, half, 1)
    given = lax.dynamic_slice_in_dim(attention, (1 - core) * half, half, 1)
    taken = lax.ppermute(given, "ctx", [(i, i ^ 1) for i in range(cycle_size)])
    pair = jnp.stack([kept, taken])
    piece = jnp.where(core == 0, pair, pair[::-1]).reshape(2 * q_rows, half)
    return project(piece, out_weight, cycle_size // 2, lax.axis_size("head"))


def solution(mesh):
    in_specs = (
        P("ctx", "head"),
        P("ctx", "head"),
        P("ctx", "head"),
        P("ctx", "head"),
        P("ctx", "head"),
        P(),
        P("head", "ctx"),
    )
    out_specs = P("head", "ctx")
    return jax.shard_map(
        on_device, mesh=mesh, in_specs=in_specs, out_specs=out_specs, check_vma=False
    )
```

```python
import functools
import math

import jax
import jax.numpy as jnp
from jax import lax
from jax.experimental import pallas as pl
from jax.experimental.pallas import tpu as pltpu
from jax.sharding import PartitionSpec as P

HD = 128
BLOCK = 64
QUANT_STEP = 1.0 / 2048.0
MASKED = -1e30
LANES = 128
MESH = pl.DeviceIdType.MESH


def hadamard_signs(size_value):
    indices = jnp.arange(size_value, dtype=jnp.int32)
    common = jnp.bitwise_and(indices[:, None], indices[None, :])
    parity = jnp.zeros((size_value, size_value), jnp.int32)
    for shift_bit in range(max(int(size_value).bit_length(), 1)):
        parity = jnp.bitwise_xor(parity, jnp.bitwise_and(jnp.right_shift(common, shift_bit), 1))
    return 1.0 - 2.0 * parity.astype(jnp.float32)


def attend_kernel(chips, heads, group, q_ref, kk_ref, vv_ref, scale_ref, pos_ref, signs_ref, a_ref,
                  q_in, s_a, s_b, out_part, in_part, out_stat, in_stat,
                  send_q, recv_q, send_part, recv_part, send_stat, recv_stat):
    me = lax.axis_index("ctx")
    chip, core = me // 2, lax.rem(me, 2)
    sibling = chip * 2 + 1 - core
    q_rows = q_ref.shape[0]
    rows, half = a_ref.shape
    ctx = s_a.shape[1]
    lane = lax.broadcasted_iota(jnp.int32, (rows, LANES), 1)

    barrier = pltpu.get_barrier_semaphore()
    for k in range(1, 2 * chips):
        other = lax.rem(me + k, 2 * chips)
        pl.semaphore_signal(barrier, inc=1, device_id={"ctx": other}, device_id_type=MESH)
    pl.semaphore_wait(barrier, 2 * chips - 1)

    def own_rows(which):
        return pl.ds(pl.multiple_of(which * q_rows, q_rows), q_rows)

    def columns(which):
        return pl.ds(pl.multiple_of(which * half, half), half)

    def query_out(k, j):
        there = core if j == 0 else 1 - core
        return pltpu.make_async_remote_copy(
            src_ref=q_ref.at[:, columns(there)], dst_ref=q_in.at[chip, own_rows(core)],
            send_sem=send_q.at[k, j], recv_sem=recv_q.at[lax.rem(chips - k, chips), j],
            device_id={"ctx": lax.rem(chip + k, chips) * 2 + there}, device_id_type=MESH)

    def query_in(k, j):
        there = core if j == 0 else 1 - core
        source = lax.rem(chip + k, chips)
        return pltpu.make_async_remote_copy(
            src_ref=q_ref.at[:, columns(core)], dst_ref=q_in.at[source, own_rows(there)],
            send_sem=send_q.at[k, j], recv_sem=recv_q.at[k, j],
            device_id={"ctx": source * 2 + there}, device_id_type=MESH)

    def part_out(k):
        return pltpu.make_async_remote_copy(
            src_ref=out_part.at[k], dst_ref=in_part.at[lax.rem(chips - k, chips)],
            send_sem=send_part.at[k], recv_sem=recv_part.at[lax.rem(chips - k, chips)],
            device_id={"ctx": lax.rem(chip + k, chips) * 2 + core}, device_id_type=MESH)

    def stat_out(k):
        return pltpu.make_async_remote_copy(
            src_ref=out_stat.at[k], dst_ref=in_stat.at[lax.rem(chips - k, chips)],
            send_sem=send_stat.at[k], recv_sem=recv_stat.at[lax.rem(chips - k, chips)],
            device_id={"ctx": lax.rem(chip + k, chips) * 2 + core}, device_id_type=MESH)

    query_out(0, 1).start()
    for k in range(1, chips):
        query_out(k, 0).start()
        query_out(k, 1).start()
    q_in[chip, own_rows(core)] = q_ref[:, columns(core)]

    def block(k, carry):
        query_in(k, 1).wait_recv()

        @pl.when(k > 0)
        def _():
            query_in(k, 0).wait_recv()

        source = lax.rem(chip + k, chips)
        limit = pos_ref[pl.ds(pl.multiple_of(source * rows, rows), rows), :]
        limit = jnp.concatenate([limit, limit], axis=0)

        def head_columns(h):
            return pl.ds(pl.multiple_of(h * HD, HD), HD)

        def scores(pair, s_ref):
            h = pair * 2
            q = jnp.concatenate([q_in[source, :, head_columns(h)], q_in[source, :, head_columns(h + 1)]], axis=0)
            g = h // group
            s = jnp.dot(jnp.concatenate([q, q], axis=1), kk_ref[g], preferred_element_type=jnp.float32)
            where = lax.broadcasted_iota(jnp.int32, (2 * rows, ctx), 1)
            s = jnp.where(where <= limit, s * scale_ref[g], MASKED)
            s_ref[...] = s
            return jnp.max(s, axis=1, keepdims=True)

        def values(pair, s_ref, top):
            h = pair * 2
            g = h // group
            p = jnp.exp2(s_ref[...] - top).astype(jnp.bfloat16)
            both = jnp.dot(p, vv_ref[g], preferred_element_type=jnp.float32)
            total = both[:, HD:]
            part = (both[:, :HD] / total).astype(jnp.bfloat16)
            out_part[k, :, head_columns(h)] = part[:rows]
            out_part[k, :, head_columns(h + 1)] = part[rows:]
            kept = jnp.where(lane == h, top[:rows], out_stat[k, 0])
            out_stat[k, 0] = jnp.where(lane == h + 1, top[rows:], kept)
            kept = jnp.where(lane == h, total[:rows], out_stat[k, 1])
            out_stat[k, 1] = jnp.where(lane == h + 1, total[rows:], kept)

        out_stat[k] = jnp.ones((2, rows, LANES), jnp.float32)
        pairs = heads // 2

        def step(i, top_a):
            top_b = scores(2 * i + 1, s_b)
            values(2 * i, s_a, top_a)
            later = scores(2 * i + 2, s_a)
            values(2 * i + 1, s_b, top_b)
            return later

        top_a = lax.fori_loop(0, pairs // 2 - 1, step, scores(0, s_a))
        top_b = scores(pairs - 1, s_b)
        values(pairs - 2, s_a, top_a)
        values(pairs - 1, s_b, top_b)

        @pl.when(k > 0)
        def _():
            part_out(k).start()
            stat_out(k).start()

        return carry

    lax.fori_loop(0, chips, block, 0)
    in_part[0] = out_part[0]
    in_stat[0] = out_stat[0]
    for k in range(1, chips):
        stat_out(chips - k).wait_recv()
        part_out(chips - k).wait_recv()
    highest = in_stat[0, 0]
    for k in range(1, chips):
        highest = jnp.maximum(highest, in_stat[k, 0])
    share = [in_stat[k, 1] * jnp.exp2(in_stat[k, 0] - highest) for k in range(chips)]
    whole = 1.0 / sum(share)
    share = [one * whole for one in share]
    for h in range(heads):
        cols = slice(h * HD, (h + 1) * HD)
        mixed = sum(in_part[k, :, cols].astype(jnp.float32) * share[k][:, h : h + 1] for k in range(chips))
        turned = jnp.dot(mixed.astype(jnp.bfloat16), signs_ref[...], preferred_element_type=jnp.float32)
        a_ref[:, cols] = (turned * (1.0 / math.sqrt(HD))).astype(jnp.bfloat16)
    query_out(0, 1).wait_send()
    for k in range(1, chips):
        query_out(k, 0).wait_send()
        query_out(k, 1).wait_send()
        part_out(k).wait_send()
        stat_out(k).wait_send()


def attend(queries, kk, vv, scale, limit, signs, chips, heads, group):
    q_rows, width = queries.shape
    kv, depth, ctx = kk.shape
    rows, half = 2 * q_rows, heads * HD
    dma = pltpu.SemaphoreType.DMA
    return pl.pallas_call(
        functools.partial(attend_kernel, chips, heads, group),
        in_specs=[pl.BlockSpec(memory_space=pltpu.VMEM)] * 6,
        out_specs=pl.BlockSpec(memory_space=pltpu.VMEM),
        out_shape=jax.ShapeDtypeStruct((rows, half), jnp.bfloat16),
        scratch_shapes=[
            pltpu.VMEM((chips, rows, half), jnp.bfloat16),
            pltpu.VMEM((2 * rows, ctx), jnp.float32),
            pltpu.VMEM((2 * rows, ctx), jnp.float32),
            pltpu.VMEM((chips, rows, half), jnp.bfloat16),
            pltpu.VMEM((chips, rows, half), jnp.bfloat16),
            pltpu.VMEM((chips, 2, rows, LANES), jnp.float32),
            pltpu.VMEM((chips, 2, rows, LANES), jnp.float32),
            dma((chips, 2)), dma((chips, 2)),
            dma((chips,)), dma((chips,)), dma((chips,)), dma((chips,)),
        ],
        compiler_params=pltpu.CompilerParams(
            collective_id=0, has_side_effects=True, vmem_limit_bytes=50 * 1024 * 1024
        ),
        cost_estimate=pl.CostEstimate(
            flops=6 * chips * rows * half * ctx, bytes_accessed=4 * q_rows * width,
            transcendentals=chips * rows * heads * ctx,
        ),
    )(queries, kk, vv, scale, limit, signs)


def project_kernel(chips, parts, a_ref, w_hbm, o_ref, w_ref, att, own, out_part, in_part,
                   w_sem, send_z, recv_z, send_core, recv_core, send_head, recv_head):
    me = lax.axis_index("ctx")
    mine = lax.axis_index("head")
    chip, core = me // 2, lax.rem(me, 2)
    sibling = chip * 2 + 1 - core
    half = a_ref.shape[1]
    columns = w_ref.shape[1]
    tile = min(512, columns)
    load = pltpu.make_async_copy(w_hbm, w_ref, w_sem)
    load.start()

    barrier = pltpu.get_barrier_semaphore()
    pl.semaphore_signal(barrier, inc=1, device_id={"ctx": sibling}, device_id_type=MESH)
    for k in range(1, chips):
        other = lax.rem(chip + k, chips) * 2 + core
        pl.semaphore_signal(barrier, inc=1, device_id={"ctx": other}, device_id_type=MESH)
    for k in range(1, parts):
        other = lax.rem(mine + k, parts)
        pl.semaphore_signal(barrier, inc=1, device_id={"head": other}, device_id_type=MESH)
    pl.semaphore_wait(barrier, chips + parts - 1)

    def to_chip(k):
        return pltpu.make_async_remote_copy(
            src_ref=a_ref, dst_ref=att.at[chip, core],
            send_sem=send_z.at[k], recv_sem=recv_z.at[chips - k],
            device_id={"ctx": lax.rem(chip + k, chips) * 2 + core}, device_id_type=MESH)

    def from_chip(k):
        source = lax.rem(chip + k, chips)
        return pltpu.make_async_remote_copy(
            src_ref=a_ref, dst_ref=att.at[source, core],
            send_sem=send_z.at[k], recv_sem=recv_z.at[k],
            device_id={"ctx": source * 2 + core}, device_id_type=MESH)

    def to_core(k):
        source = lax.rem(chip + k, chips)
        return pltpu.make_async_remote_copy(
            src_ref=a_ref if k == 0 else att.at[source, core], dst_ref=att.at[source, core],
            send_sem=send_core.at[k], recv_sem=recv_core.at[k],
            device_id={"ctx": sibling}, device_id_type=MESH)

    def from_core(k):
        source = lax.rem(chip + k, chips)
        return pltpu.make_async_remote_copy(
            src_ref=a_ref, dst_ref=att.at[source, 1 - core],
            send_sem=send_core.at[k], recv_sem=recv_core.at[k],
            device_id={"ctx": sibling}, device_id_type=MESH)

    def to_part(k):
        block = lax.rem(chip + k, chips)
        return pltpu.make_async_remote_copy(
            src_ref=out_part.at[k], dst_ref=in_part.at[mine],
            send_sem=send_head.at[k], recv_sem=recv_head.at[mine],
            device_id={"head": block}, device_id_type=MESH)

    for k in range(1, chips):
        to_chip(k).start()
    to_core(0).start()
    att[chip, core] = a_ref[...]
    load.wait()
    for k in range(chips):
        if k > 0:
            from_chip(k).wait_recv()
            to_core(k).start()
        from_core(k).wait_recv()
        block = lax.rem(chip + k, chips)

        @pl.loop(0, columns // tile)
        def _(t):
            cols = pl.ds(pl.multiple_of(t * tile, tile), tile)
            product = jnp.dot(att[block, 0], w_ref[:half, cols], preferred_element_type=jnp.float32)
            product += jnp.dot(att[block, 1], w_ref[half:, cols], preferred_element_type=jnp.float32)
            out_part[k, :, cols] = product.astype(jnp.bfloat16)

            @pl.when(block == mine)
            def _():
                own[:, cols] = product

        @pl.when(block != mine)
        def _():
            to_part(k).start()

    total = own[...]
    for k in range(1, parts):
        source = lax.rem(mine + k, parts)
        pltpu.make_async_remote_copy(
            src_ref=out_part.at[0], dst_ref=in_part.at[source],
            send_sem=send_head.at[0], recv_sem=recv_head.at[source],
            device_id={"head": source}, device_id_type=MESH).wait_recv()
        total = total + in_part[source].astype(jnp.float32)
    o_ref[...] = total.astype(o_ref.dtype)
    for k in range(1, chips):
        to_chip(k).wait_send()
    for k in range(chips):
        to_core(k).wait_send()

        @pl.when(lax.rem(chip + k, chips) != mine)
        def _():
            to_part(k).wait_send()


def project(piece, out_weight, chips, parts):
    rows, half = piece.shape
    depth, columns = out_weight.shape
    dma = pltpu.SemaphoreType.DMA
    return pl.pallas_call(
        functools.partial(project_kernel, chips, parts),
        out_shape=jax.ShapeDtypeStruct((rows, columns), jnp.bfloat16),
        in_specs=[pl.BlockSpec(memory_space=pltpu.VMEM), pl.BlockSpec(memory_space=pl.ANY)],
        out_specs=pl.BlockSpec(memory_space=pltpu.VMEM),
        scratch_shapes=[
            pltpu.VMEM((depth, columns), jnp.bfloat16),
            pltpu.VMEM((chips, 2, rows, half), jnp.bfloat16),
            pltpu.VMEM((rows, columns), jnp.float32),
            pltpu.VMEM((chips, rows, columns), jnp.bfloat16),
            pltpu.VMEM((parts, rows, columns), jnp.bfloat16),
            dma,
            dma((chips,)), dma((chips,)), dma((chips,)), dma((chips,)),
            dma((chips,)), dma((parts,)),
        ],
        compiler_params=pltpu.CompilerParams(
            collective_id=1, has_side_effects=True, vmem_limit_bytes=50 * 1024 * 1024
        ),
        cost_estimate=pl.CostEstimate(
            flops=2 * chips * rows * depth * columns, bytes_accessed=2 * depth * columns, transcendentals=0
        ),
    )(piece, out_weight)


def on_device(queries, key_codes, value_codes, key_scales, value_scales, positions, out_weight):
    kv_local = key_scales.shape[1]
    ctx_local = key_codes.shape[0]
    cycle_index = lax.axis_index("ctx")
    cycle_size = lax.axis_size("ctx")
    chip, core = cycle_index // 2, cycle_index % 2
    heads = queries.shape[1] // HD // 2
    kv = max(kv_local // 2, 1)
    swap = [(i, i ^ 1) for i in range(cycle_size)]

    def both_cores(first, second):
        width = first.shape[1] // kv_local * kv

        def part(value, which):
            return lax.dynamic_slice_in_dim(value, which * (width if kv_local > 1 else 0), width, 1)

        kept = jnp.concatenate([part(first, core), part(second, core)], axis=1)
        given = jnp.concatenate([part(first, 1 - core), part(second, 1 - core)], axis=1)
        taken = lax.ppermute(given, "ctx", swap)
        low = jnp.where(core == 0, kept, taken)
        high = jnp.where(core == 0, taken, kept)
        together = jnp.concatenate([low, high], axis=0)
        return together[:, :width], together[:, width:]

    ctx = 2 * ctx_local
    signs = hadamard_signs(HD).astype(jnp.bfloat16)
    keys, values = both_cores(key_codes, value_codes)
    key_scales, value_scales = both_cores(key_scales.astype(jnp.float32), value_scales.astype(jnp.float32))
    turned = jnp.einsum(
        "cgd,de->gec", keys.reshape(ctx, kv, HD), signs, preferred_element_type=jnp.float32
    )
    coarse = jnp.floor(turned * (1.0 / 128.0)) * 128.0
    kk = jnp.concatenate([coarse, turned - coarse], axis=1).astype(jnp.bfloat16)
    scale = jnp.repeat(key_scales, BLOCK, axis=0).T[:, None, :]
    scale = scale * (QUANT_STEP / HD * math.log2(math.e))
    value_factor = jnp.repeat(value_scales, BLOCK, axis=0) * QUANT_STEP
    scaled = values.reshape(ctx, kv, HD).astype(jnp.float32) * value_factor[..., None]
    vv = jnp.concatenate([scaled, jnp.ones_like(scaled)], axis=2).astype(jnp.bfloat16)
    vv = vv.transpose(1, 0, 2)
    limit = (positions - chip * ctx)[:, None]
    piece = attend(queries, kk, vv, scale, limit, signs, cycle_size // 2, heads, heads // kv)
    return project(piece, out_weight, cycle_size // 2, lax.axis_size("head"))


def solution(mesh):
    in_specs = (
        P("ctx", "head"),
        P("ctx", "head"),
        P("ctx", "head"),
        P("ctx", "head"),
        P("ctx", "head"),
        P(),
        P("head", "ctx"),
    )
    out_specs = P("head", "ctx")
    return jax.shard_map(
        on_device, mesh=mesh, in_specs=in_specs, out_specs=out_specs, check_vma=False
    )
```
